1024 devices in a mesh: sens: 64 (over z_hi, x, core), pts: 16 (over y, z_lo).
Axes of the slice: x: 8, y: 8, z: 8 (z_hi: 4, z_lo: 2; z = z_hi * 2 + z_lo), core: 2. Of those that a mesh axis runs over, the one named last changes fastest.
Arguments:
- observed: float32 [128, 2, 420], P('sens'), may hold values from -8 to 8
- spectra: bfloat16 [2, 211, 128, 12288], P(None, None, 'sens', 'pts'), may hold values from -1 to 1
- prior_factor: bfloat16 [12288, 768], P('pts'), may hold values from -0.21875 to 0.21875
- noise_cov: bfloat16 [4, 420, 420], replicated, may hold values from -1 to 1.25
- noise_inv: bfloat16 [4, 420, 420], replicated, may hold values from -1 to 1.25
- sensor_block: int32 [128], P('sens'), may hold values from 0 to 3
- window_len: int32 [128], P('sens'), may hold values from 105 to 420, as said below
Outputs:
- solution: float32 [128, 2, 420], P('sens')
- residual: float32 [128, 2, 420], P('sens')
The draws below stay inside these ranges and needn't reach their ends.
Inputs may be any that keep to these rules, and one draw needn't show every extreme that they name: `window_len`: some sensor has all 420 samples active.
All inputs are finite; a program needn't handle non-finite values.
Results may differ from the reference program's by a relative error of at most 0.012.
The reference program's roundings to bfloat16 on the way count: a program that leaves them out, or rounds other values in their place, can miss the bound.
Values may be sent and summed in bfloat16 or wider, within the bound.
A program may use at most 64 MiB of HBM per device.

```python
import jax
import jax.numpy as jnp
from jax import lax

NT = 420
F = 211
S = 128
PTS_DEV = 768
PTS = 12288
RHS = 2
NB = 4
N_PTS = 16


def noise_table(key):
    key_off, key_diag = jax.random.split(key)
    bound = 0.75 / NT
    offdiag = jax.random.uniform(key_off, (NB, NT, NT), jnp.float32, -bound, bound)
    offdiag = 0.5 * (offdiag + jnp.swapaxes(offdiag, 1, 2))
    diagonal = jax.random.uniform(key_diag, (NB, NT), jnp.float32, 0.8, 1.25)
    identity = jnp.eye(NT, dtype=jnp.float32)
    return offdiag * (1.0 - identity)[None] + diagonal[:, :, None] * identity[None]


def draw_observed(key, part):
    key = jax.random.fold_in(key, 11)
    values = jnp.clip(jax.random.normal(key, (S, RHS, NT), jnp.float32), -4.0, 4.0)
    ramp = 0.6 + 1.2 * jnp.arange(S, dtype=jnp.float32) / max(S - 1, 1)
    return values * ramp[:, None, None]


def draw_spectra(key, part):
    key = jax.random.fold_in(key, 12)
    factor = 0.7 * (S * PTS) ** (-0.25)
    values = jnp.clip(jax.random.normal(key, (2, F, S, PTS), jnp.float32), -5.0, 5.0)
    return (values * factor).astype(jnp.bfloat16)


def draw_noise_cov(key, part):
    key = jax.random.fold_in(key, 13)
    return noise_table(key).astype(jnp.bfloat16)


def draw_noise_inv(key, part):
    key = jax.random.fold_in(key, 14)
    return noise_table(key).astype(jnp.bfloat16)


def draw_window_len(key, part):
    key = jax.random.fold_in(key, 15)
    key_len, key_full = jax.random.split(key)
    lengths = jax.random.randint(key_len, (S,), NT // 4, NT + 1, jnp.int32)
    chosen = jax.random.randint(key_full, (), 0, S, jnp.int32)
    return jnp.where(jnp.arange(S, dtype=jnp.int32) == chosen, NT, lengths).astype(jnp.int32)


def touch_ends(array, rng, low, largest):
    spot = [jax.random.randint(jax.random.fold_in(rng, axis), (), 0, length) for axis, length in enumerate(array.shape)]
    main_axis = array.shape.index(max(array.shape))
    neighbour = spot[:main_axis] + [(spot[main_axis] + 1) % array.shape[main_axis]] + spot[main_axis + 1:]
    return array.at[tuple(spot)].set(low).at[tuple(neighbour)].set(largest)


def shard_levels(rng, shape, pieces, smallest, largest):
    factor_of, own = 1.0, jax.random.fold_in(rng, 6)
    for dim, blocks in pieces:
        steps = jnp.exp(jax.random.uniform(jax.random.fold_in(own, dim), (blocks,), jnp.float32, smallest / len(pieces), largest / len(pieces)))
        factor_of = factor_of * jnp.repeat(steps, shape[dim] // blocks).reshape([-1 if axis == dim else 1 for axis in range(len(shape))])
    return factor_of


def noise(own_key, dims, width, reach, cuts=(), kind=jnp.bfloat16):
    drawn = width * jax.random.normal(own_key, dims, jnp.float32)
    if cuts:
        drawn = drawn * shard_levels(own_key, dims, cuts, -0.22, 0.18)
    return jnp.clip(drawn, -reach, reach).astype(kind)


def setup_inputs(seed: int = 0) -> dict:
    seeds = jax.random.split(jax.random.key(seed), 8)
    observed = draw_observed(jax.random.fold_in(seeds[7], 71), 0)
    spectra = draw_spectra(jax.random.fold_in(seeds[7], 71), 0)
    prior_factor = noise(seeds[2], (PTS, PTS_DEV), PTS_DEV ** -0.5, 0.21875, ((0, 16),))
    noise_cov = draw_noise_cov(jax.random.fold_in(seeds[7], 71), 0)
    noise_inv = draw_noise_inv(jax.random.fold_in(seeds[7], 71), 0)
    sensor_block = touch_ends(jax.random.randint(seeds[5], (S,), 0, NB), jax.random.fold_in(seeds[5], 1), 0, NB - 1).astype(jnp.int32)
    window_len = draw_window_len(jax.random.fold_in(seeds[7], 71), 0)
    return dict(observed=observed, spectra=spectra, prior_factor=prior_factor, noise_cov=noise_cov, noise_inv=noise_inv, sensor_block=sensor_block, window_len=window_len)


def apply_table(matrix_set, field_in, sensor_block):
    tables = matrix_set[sensor_block].astype(jnp.float32)
    return jnp.einsum('stu,sru->srt', tables, field_in, precision=lax.Precision.HIGHEST)


def reference(observed, spectra, prior_factor, noise_cov, noise_inv, sensor_block, window_len):
    time_index = jnp.arange(NT, dtype=jnp.int32)
    window_mask = (time_index[None, :] < window_len[:, None]).astype(jnp.float32)
    start_res = observed * window_mask[:, None, :]
    direction = window_mask[:, None, :] * apply_table(noise_inv, start_res, sensor_block)
    inner_total = jnp.sum(start_res * direction, axis=(0, 2))
    cov_image = window_mask[:, None, :] * apply_table(noise_cov, direction, sensor_block)
    spectrum = jnp.fft.rfft(direction, axis=-1)
    hat_re = jnp.real(spectrum).astype(jnp.bfloat16)
    hat_im = jnp.imag(spectrum).astype(jnp.bfloat16)

    def adjoint_bin(index):
        spec_re = spectra[0, index]
        spec_im = spectra[1, index]
        vec_re = hat_re[:, :, index].T
        vec_im = hat_im[:, :, index].T
        part_re = jnp.dot(vec_re, spec_re, preferred_element_type=jnp.float32) + jnp.dot(vec_im, spec_im, preferred_element_type=jnp.float32)
        part_im = jnp.dot(vec_im, spec_re, preferred_element_type=jnp.float32) - jnp.dot(vec_re, spec_im, preferred_element_type=jnp.float32)
        return jnp.stack([part_re, part_im])

    adjoint = jnp.moveaxis(lax.map(adjoint_bin, jnp.arange(F)), 1, 0).astype(jnp.bfloat16)
    blocks = prior_factor.astype(jnp.float32).reshape(N_PTS, PTS_DEV, PTS_DEV)
    adj_blocks = adjoint.astype(jnp.float32).reshape(2, F, RHS, N_PTS, PTS_DEV)
    weighted = jnp.einsum('xfrja,jab->xfrjb', adj_blocks, blocks, precision=lax.Precision.HIGHEST)
    weighted_low = lax.optimization_barrier(weighted.astype(jnp.bfloat16)).astype(jnp.float32)
    spread = jnp.einsum('xfrjb,jab->xfrja', weighted_low, blocks, precision=lax.Precision.HIGHEST)
    spread = spread.astype(jnp.bfloat16).reshape(2, F, RHS, PTS)

    def forward_bin(index):
        spec_re = spectra[0, index]
        spec_im = spectra[1, index]
        src_re = spread[0, index].T
        src_im = spread[1, index].T
        out_re = jnp.dot(spec_re, src_re, preferred_element_type=jnp.float32) - jnp.dot(spec_im, src_im, preferred_element_type=jnp.float32)
        out_im = jnp.dot(spec_re, src_im, preferred_element_type=jnp.float32) + jnp.dot(spec_im, src_re, preferred_element_type=jnp.float32)
        return jnp.stack([out_re, out_im])

    forward = lax.map(forward_bin, jnp.arange(F))
    fwd_re = jnp.transpose(forward[:, 0], (1, 2, 0))
    fwd_im = jnp.transpose(forward[:, 1], (1, 2, 0))
    signal = jnp.fft.irfft(lax.complex(fwd_re, fwd_im), n=NT, axis=-1)
    image = cov_image + window_mask[:, None, :] * signal
    curvature = jnp.sum(direction * image, axis=(0, 2))
    step_size = inner_total / curvature
    solution = step_size[None, :, None] * direction
    residual = start_res - step_size[None, :, None] * image
    return (solution, residual)
```

```python
import functools
import math

import jax
import jax.numpy as jnp
import numpy as np
from jax import lax
from jax.experimental import pallas as pl
from jax.experimental.pallas import tpu as pltpu
from jax.sharding import PartitionSpec as P

MESH = pl.DeviceIdType.MESH
NT, F, PD, NB = 420, 211, 768, 4
NS, NP = 64, 16
FB = 4
NC = -(-F // FB)
TP = 432
FIRST = 40
f32, bf16 = jnp.float32, jnp.bfloat16


def chunk_of(dev):
    return (dev * NC + NS - 1) // NS


def is_owner(dev):
    c = chunk_of(dev)
    return (c * NS) // NC == dev


@functools.cache
def tables():
    t = np.arange(NT)
    fwd = np.zeros((2, FB, NS, NT))
    inv = np.zeros((NS, 2, FB, NT))
    for dev in range(NS):
        c = -(-dev * NC // NS)
        if (c * NS) // NC != dev or c >= NC:
            continue
        for f in range(FB):
            bin_ = FB * c + f
            if bin_ >= F:
                continue
            phase = (t * bin_) % NT
            cosine = np.cos(2 * math.pi * phase / NT)
            sine = np.where(phase % (NT // 2) == 0, 0.0, np.sin(2 * math.pi * phase / NT))
            weight = (1.0 if bin_ in (0, NT // 2) else 2.0) / NT
            fwd[0, f, dev], fwd[1, f, dev] = cosine, -sine
            inv[dev, 0, f], inv[dev, 1, f] = cosine * weight, -sine * weight
    fwd = fwd.reshape(2 * FB * NS, NT)
    inv = inv.reshape(4, 16, 8, NT).transpose(0, 2, 1, 3).reshape(512, NT)
    gt = np.zeros((128, 16))
    mask = np.zeros((16, 128))
    for xk in range(2):
        for x in range(2):
            for f in range(FB):
                for s in range(2):
                    mask[xk * 8 + f * 2 + s, xk * 32 + x * 16 + f * 4 + s * 2 :][:2] = 1
                    for r in range(2):
                        m = xk * 32 + x * 16 + f * 4 + s * 2 + r
                        j = f * 4 + (x if xk == 0 else 1 - x) * 2 + r
                        gt[m, j] = 1 if xk == 0 or x == 1 else -1
    rep = np.tile(np.eye(16), (1, 32))
    pick = np.zeros((128, 512))
    for row in range(128):
        pick[row, (row // 4) * 16 : (row // 4) * 16 + 16] = 1
    fold = np.zeros((8, 128))
    for row in range(128):
        fold[row % 4, row] = 1
    return dict(
        fwd=fwd.astype(np.float32),
        inv=inv.astype(np.float32),
        gt=gt.astype(np.float32),
        g=gt.T.astype(np.float32),
        mask=mask.astype(np.float32),
        rep=rep.astype(np.float32),
        pick=pick.astype(np.float32),
        fold=fold.astype(np.float32),
    )


def parts3(x):
    a = x.astype(bf16).astype(f32)
    b = (x - a).astype(bf16).astype(f32)
    return a, b, x - a - b


def parts2(x):
    a = x.astype(bf16)
    return a, (x - a.astype(f32)).astype(bf16)


def nt_dot(a, b):
    return lax.dot_general(a, b, (((1,), (1,)), ((), ())), preferred_element_type=f32)


def kernel(
    wl, sb, obs, kx, prior, ninv, ncov, dft, idft, gt, g, mask16, rep, pick, fold,
    sol, res,
    kk, prior_v, ninv_v, ncov_v, dft_v, idft_v, tsel, hsend, hrecv, vsend, vrecv, psend, precv, otmp,
    lsem, ksend, krecv, hss, hrs, vss, vrs, pss, prs,
):
    me, mp = lax.axis_index("sens"), lax.axis_index("pts")
    mine = is_owner(me)
    my_chunk = chunk_of(me)

    locals_ = [
        pltpu.make_async_copy(ninv, ninv_v.at[pl.ds(0, NT)], lsem.at[0]),
        pltpu.make_async_copy(dft, dft_v, lsem.at[1]),
        pltpu.make_async_copy(ncov, ncov_v.at[pl.ds(0, NT)], lsem.at[2]),
        pltpu.make_async_copy(prior, prior_v, lsem.at[3]),
        pltpu.make_async_copy(idft, idft_v, lsem.at[4]),
    ]
    for copy in locals_:
        copy.start()

    barrier = pltpu.get_barrier_semaphore()

    @pl.loop(1, NS)
    def _(k):
        pl.semaphore_signal(barrier, inc=1, device_id={"sens": lax.rem(me + k, NS)}, device_id_type=MESH)

    @pl.loop(1, NP)
    def _(k):
        pl.semaphore_signal(barrier, inc=1, device_id={"pts": lax.rem(mp + k, NP)}, device_id_type=MESH)

    pl.semaphore_wait(barrier, NS + NP - 2)

    def k_copy(peer):
        return pltpu.make_async_remote_copy(
            src_ref=kx.at[jnp.minimum(chunk_of(peer), NC - 1)],
            dst_ref=kk.at[pl.ds(pl.multiple_of(me * 16, 16), 16)],
            send_sem=ksend.at[peer],
            recv_sem=krecv.at[me],
            device_id={"sens": peer},
            device_id_type=MESH,
        )

    def k_arrived(peer):
        return pltpu.make_async_copy(
            kx.at[0], kk.at[pl.ds(pl.multiple_of(peer * 16, 16), 16)], krecv.at[peer]
        )

    def row_copy(src, dst, ss, rs, peer):
        return pltpu.make_async_remote_copy(
            src_ref=src.at[peer],
            dst_ref=dst.at[me],
            send_sem=ss.at[peer],
            recv_sem=rs.at[me],
            device_id={"sens": peer},
            device_id_type=MESH,
        )

    def row_arrived(src, dst, rs, peer):
        return pltpu.make_async_copy(src.at[peer], dst.at[peer], rs.at[peer])

    def start_k(k):
        peer = lax.rem(me + k, NS)

        @pl.when(is_owner(peer))
        def _():
            k_copy(peer).start()

    own = pltpu.make_async_copy(
        kx.at[jnp.minimum(my_chunk, NC - 1)], kk.at[pl.ds(pl.multiple_of(me * 16, 16), 16)], krecv.at[me]
    )

    @pl.when(mine)
    def _():
        own.start()

    pl.loop(1, FIRST)(start_k)

    time = lax.broadcasted_iota(jnp.int32, (2, NT), 1)
    masks = [(time < wl[s]).astype(f32) for s in range(2)]
    start = [obs[s] * masks[s] for s in range(2)]

    def select(table_v):
        @pl.loop(0, TP // 16)
        def _(i):
            rows = pl.ds(pl.multiple_of(i * 16, 16), 16)
            block = table_v[rows].astype(f32)
            which = lax.broadcasted_iota(jnp.int32, block.shape, 1)
            for s in range(2):
                tsel[s, rows, :] = jnp.where(which == sb[s], block, 0.0).sum(axis=1).astype(bf16)

    def apply_selected(x):
        out = []
        for s in range(2):
            a, b, c = parts3(x[s])
            stacked = jnp.concatenate([a, b, c, jnp.zeros_like(a)], axis=0).astype(bf16)
            y = nt_dot(stacked, tsel[s])[:, :NT]
            out.append(masks[s] * (y[0:2] + y[2:4] + y[4:6]))
        return out

    locals_[0].wait()
    select(ninv_v)
    direction = apply_selected(start)

    locals_[1].wait()
    d4 = jnp.concatenate(direction, axis=0)
    da, db, dc = parts3(d4)
    d128 = jnp.concatenate([da] * 8 + [db] * 8 + [dc] * 8 + [jnp.zeros_like(da)] * 8, axis=0).astype(bf16)
    lane = lax.broadcasted_iota(jnp.int32, (NS, 128), 1)
    hat = jnp.zeros((NS, 128), f32)
    for part, table in enumerate(parts2(dft_v[...])):
        full = nt_dot(table, d128)
        picked = jnp.zeros((NS, 128), f32)
        for xf in range(8):
            picked += jnp.where((lane % 32) // 4 == xf, full[xf * NS : (xf + 1) * NS], 0.0)
        hat += picked + pltpu.roll(picked, 96, 1)
        if part == 0:
            hat += pltpu.roll(picked, 64, 1)
    hat = jnp.where(lane < 32, hat, 0.0)
    hsend[...] = hat.reshape(NS, 1, 128)

    @pl.loop(1, NS)
    def _(k):
        peer = lax.rem(me + k, NS)

        @pl.when(is_owner(peer))
        def _():
            row_copy(hsend, hrecv, hss, hrs, peer).start()

    pl.loop(FIRST, NS)(start_k)
    hrecv[me] = hsend[me]

    locals_[2].wait()
    select(ncov_v)
    cov = apply_selected(direction)
    inner = sum(jnp.sum(start[s] * direction[s], axis=1, keepdims=True) for s in range(2))
    curve = sum(jnp.sum(cov[s] * direction[s], axis=1, keepdims=True) for s in range(2))
    for copy in locals_[3:]:
        copy.wait()

    lane1 = lax.broadcasted_iota(jnp.int32, (1, 128), 1)
    known = jnp.zeros((1, 128), f32)
    for at, value in ((34, inner[0:1]), (35, inner[1:2]), (36, curve[0:1]), (37, curve[1:2])):
        known += jnp.where(lane1 == at, value, 0.0)

    @pl.when(mine)
    def _():
        @pl.loop(1, NS)
        def _(k):
            peer = lax.rem(me + k, NS)
            row_arrived(hsend, hrecv, hrs, peer).wait()

        rows = hrecv[...]
        twice = rows + pltpu.roll(rows.reshape(NS, 128), 32, 1).reshape(NS, 1, 128)
        z = (jnp.broadcast_to(twice, (NS, 16, 128)) * mask16[...][None]).reshape(NS * 16, 128).astype(bf16)
        h = nt_dot(g[...].astype(bf16), z).astype(bf16)

        @pl.loop(0, NS)
        def _(k):
            k_arrived(lax.rem(me + k, NS)).wait()

        adjoint = jnp.dot(h, kk[...], preferred_element_type=f32).astype(bf16)
        weighted = jnp.dot(adjoint, prior_v[...], preferred_element_type=f32).astype(bf16)
        spread = nt_dot(weighted, prior_v[...]).astype(bf16)
        spread = jnp.dot(gt[...].astype(bf16), spread, preferred_element_type=f32).astype(bf16)
        cross = nt_dot(kk[...], spread)
        folded = (cross.reshape(NS, 16, 128) * mask16[...][None]).sum(axis=1)
        folded = folded + pltpu.roll(folded, 96, 1)
        folded = jnp.where(lane < 32, folded, 0.0)
        bins = FB * my_chunk + (lane % 16) // 4
        weight = jnp.where((bins == 0) | (bins == NT // 2), 1.0, 2.0) / NT
        terms = folded * rows.reshape(NS, 128) * weight
        for r in range(2):
            value = jnp.sum(jnp.where(lane % 2 == r, terms, 0.0), keepdims=True)
            folded = folded + jnp.where(lane == 32 + r, value, 0.0)
        vsend[...] = (folded + known).reshape(NS, 1, 128)

    @pl.when(jnp.logical_not(mine))
    def _():
        vsend[...] = jnp.broadcast_to(known[None], (NS, 1, 128))

    @pl.loop(1, NS)
    def _(k):
        row_copy(vsend, vrecv, vss, vrs, lax.rem(me + k, NS)).start()

    vrecv[me] = vsend[me]

    @pl.loop(1, NS)
    def _(k):
        row_arrived(vsend, vrecv, vrs, lax.rem(me + k, NS)).wait()

    got = vrecv[...].reshape(NS, 128)
    total = jnp.sum(got, axis=0, keepdims=True)
    got = jnp.where(lane < 32, got, 0.0)
    packed = got[0:16]
    for q in range(1, 4):
        packed += pltpu.roll(got[16 * q : 16 * q + 16], 32 * q, 1)
    row16 = lax.broadcasted_iota(jnp.int32, (16, 128), 0)
    lane16 = lax.broadcasted_iota(jnp.int32, (16, 128), 1)
    spare = jnp.broadcast_to(pltpu.roll(jnp.where((lane1 == 32) | (lane1 == 33), total, 0.0), 64, 1), (16, 128))
    packed = jnp.where((row16 == 15) & (lane16 >= 96), spare, packed)
    psend[...] = packed
    precv[mp] = packed

    def p_copy(peer):
        return pltpu.make_async_remote_copy(
            src_ref=psend,
            dst_ref=precv.at[mp],
            send_sem=pss.at[peer],
            recv_sem=prs.at[mp],
            device_id={"pts": peer},
            device_id_type=MESH,
        )

    def p_arrived(peer):
        return pltpu.make_async_copy(psend, precv.at[peer], prs.at[peer])

    @pl.loop(1, NP)
    def _(k):
        p_copy(lax.rem(mp + k, NP)).start()

    @pl.loop(1, NP)
    def _(k):
        p_arrived(lax.rem(mp + k, NP)).wait()

    forward = jnp.sum(precv[...], axis=0)

    def at_lane(x, n):
        return jnp.sum(jnp.where(lax.broadcasted_iota(jnp.int32, x.shape, 1) == n, x, 0.0), axis=1, keepdims=True)

    last = forward[15:16]
    step = [at_lane(total, 34 + r) / (at_lane(last, 96 + r) + at_lane(total, 36 + r)) for r in range(2)]
    fa = forward.astype(bf16)
    fb = (forward - fa.astype(f32)).astype(bf16)
    spread_out = []
    for part in (fa, fb):
        tiled = lax.dot_general(part, rep[...].astype(bf16), (((0,), (0,)), ((), ())), preferred_element_type=f32)
        tiled = (tiled * pick[...]).astype(bf16)
        spread_out.append(jnp.dot(fold[...].astype(bf16), tiled, preferred_element_type=f32)[0:4])
    both = jnp.concatenate(spread_out, axis=0).astype(bf16)
    hi, lo = (jnp.dot(both, table, preferred_element_type=f32) for table in parts2(idft_v[...]))
    signal = hi[0:4] + hi[4:8] + lo[0:4]
    row2 = lax.broadcasted_iota(jnp.int32, (2, NT), 0)
    size = jnp.where(row2 == 0, step[0], step[1])
    for s in range(2):
        image = cov[s] + masks[s] * signal[2 * s : 2 * s + 2]
        sol[s] = size * direction[s]
        res[s] = start[s] - size * image

    @pl.loop(1, NS)
    def _(k):
        peer = lax.rem(me + k, NS)

        @pl.when(is_owner(peer))
        def _():
            k_copy(peer).wait_send()
            row_copy(hsend, hrecv, hss, hrs, peer).wait_send()

        row_copy(vsend, vrecv, vss, vrs, peer).wait_send()

    @pl.loop(1, NP)
    def _(k):
        p_copy(lax.rem(mp + k, NP)).wait_send()


def shards(observed, spectra, prior_factor, noise_cov, noise_inv, sensor_block, window_len):
    c = tables()
    kx = jnp.pad(spectra, ((0, 0), (0, NC * FB - F), (0, 0), (0, 0)))
    kx = kx.reshape(2, NC, FB, 2, PD).transpose(1, 0, 2, 3, 4).reshape(NC, 16, PD)
    vmem, smem, any_ = (pl.BlockSpec(memory_space=m) for m in (pltpu.VMEM, pltpu.SMEM, pl.ANY))
    dma = pltpu.SemaphoreType.DMA
    out = jax.ShapeDtypeStruct((2, 2, NT), f32)
    return pl.pallas_call(
        kernel,
        out_shape=(out, out),
        in_specs=[smem, smem, vmem] + [any_] * 6 + [vmem] * 6,
        out_specs=(vmem, vmem),
        scratch_shapes=[
            pltpu.VMEM((NS * 16, PD), bf16),
            pltpu.VMEM((PD, PD), bf16),
            pltpu.VMEM((TP, NB, NT), bf16),
            pltpu.VMEM((TP, NB, NT), bf16),
            pltpu.VMEM((512, NT), f32),
            pltpu.VMEM((512, NT), f32),
            pltpu.VMEM((2, TP, NT), bf16),
            pltpu.VMEM((NS, 1, 128), f32),
            pltpu.VMEM((NS, 1, 128), f32),
            pltpu.VMEM((NS, 1, 128), f32),
            pltpu.VMEM((NS, 1, 128), f32),
            pltpu.VMEM((16, 128), f32),
            pltpu.VMEM((NP, 16, 128), f32),
            pltpu.VMEM((8, 128), f32),
            dma((5,)),
            dma((NS,)), dma((NS,)), dma((NS,)), dma((NS,)), dma((NS,)), dma((NS,)),
            dma((NP,)), dma((NP,)),
        ],
        compiler_params=pltpu.CompilerParams(
            collective_id=0, has_side_effects=True, vmem_limit_bytes=48 << 20
        ),
        cost_estimate=pl.CostEstimate(flops=10**10, bytes_accessed=10**7, transcendentals=0),
    )(
        window_len, sensor_block, observed, kx, prior_factor,
        noise_inv.transpose(1, 0, 2), noise_cov.transpose(1, 0, 2),
        c["fwd"], c["inv"], c["gt"], c["g"], c["mask"], c["rep"], c["pick"], c["fold"],
    )


def solution(mesh):
    placed = (
        P("sens", None, None),
        P(None, None, "sens", "pts"),
        P("pts", None),
        P(),
        P(),
        P("sens"),
        P("sens"),
    )
    return jax.shard_map(
        shards,
        mesh=mesh,
        in_specs=placed,
        out_specs=(P("sens", None, None), P("sens", None, None)),
        check_vma=False,
    )
```

```python
import functools
import math

import jax
import jax.numpy as jnp
import numpy as np
from jax import lax
from jax.experimental import pallas as pl
from jax.experimental.pallas import tpu as pltpu
from jax.sharding import PartitionSpec as P

MESH = pl.DeviceIdType.MESH
NT, F, PD, NB = 420, 211, 768, 4
NS, NP = 64, 16
FB = 4
NC = -(-F // FB)
TP = 432
FIRST = 40
f32, bf16 = jnp.float32, jnp.bfloat16


def chunk_of(dev):
    return (dev * NC + NS - 1) // NS


def first_bin(c):
    return jnp.minimum(FB * c, F - FB)


def is_owner(dev):
    return chunk_of(dev + 1) != chunk_of(dev)


@functools.cache
def tables():
    t = np.arange(NT)
    fwd = np.zeros((2, FB, NS, NT))
    inv = np.zeros((NS, 2, FB, NT))
    for dev in range(NS):
        c = -(-dev * NC // NS)
        if (c * NS) // NC != dev or c >= NC:
            continue
        for f in range(FB):
            bin_ = min(FB * c, F - FB) + f
            if bin_ < FB * c:
                continue
            phase = (t * bin_) % NT
            cosine = np.cos(2 * math.pi * phase / NT)
            sine = np.where(phase % (NT // 2) == 0, 0.0, np.sin(2 * math.pi * phase / NT))
            weight = (1.0 if bin_ in (0, NT // 2) else 2.0) / NT
            fwd[0, f, dev], fwd[1, f, dev] = cosine, -sine
            inv[dev, 0, f], inv[dev, 1, f] = cosine * weight, -sine * weight
    fwd = fwd.reshape(2 * FB * NS, NT)
    inv = inv.reshape(4, 16, 8, NT).transpose(0, 2, 1, 3).reshape(512, NT)
    gt = np.zeros((128, 16))
    mask = np.zeros((16, 128))
    for xk in range(2):
        for x in range(2):
            for f in range(FB):
                for s in range(2):
                    mask[xk * 8 + f * 2 + s, xk * 32 + x * 16 + f * 4 + s * 2 :][:2] = 1
                    for r in range(2):
                        m = xk * 32 + x * 16 + f * 4 + s * 2 + r
                        j = f * 4 + (x if xk == 0 else 1 - x) * 2 + r
                        gt[m, j] = 1 if xk == 0 or x == 1 else -1
    rep = np.tile(np.eye(16), (1, 32))
    pick = np.zeros((128, 512))
    for row in range(128):
        pick[row, (row // 4) * 16 : (row // 4) * 16 + 16] = 1
    fold = np.zeros((8, 128))
    for row in range(128):
        fold[row % 4, row] = 1
    small = np.zeros((312, 512))
    small[0:128] = pick
    small[128:144] = rep
    small[144:160, :128] = gt.T
    small[160:176, :128] = mask
    small[176:304, :16] = gt
    small[304:312, :128] = fold
    return [a.astype(np.float32) for a in (fwd, inv, small)]


def parts3(x):
    a = x.astype(bf16).astype(f32)
    b = (x - a).astype(bf16).astype(f32)
    return a, b, x - a - b


def parts2(x):
    a = x.astype(bf16)
    return a, (x - a.astype(f32)).astype(bf16)


def nt_dot(a, b):
    return lax.dot_general(a, b, (((1,), (1,)), ((), ())), preferred_element_type=f32)


def kernel(
    wl, sb, obs, kx, prior, ninv, ncov, dft, idft, small,
    sol, res,
    raw, kk, prior_v, ninv_v, ncov_v, dft_v, idft_v, tsel, hsend, hrecv, vsend, vrecv, psend, precv, small_v,
    lsem, ksend, krecv, hss, hrs, vss, vrs, pss, prs,
):
    me, mp = lax.axis_index("sens"), lax.axis_index("pts")
    mine = is_owner(me)
    my_chunk = chunk_of(me)

    locals_ = [
        pltpu.make_async_copy(ninv, ninv_v.at[pl.ds(0, NT)], lsem.at[0]),
        pltpu.make_async_copy(dft, dft_v, lsem.at[1]),
        pltpu.make_async_copy(ncov, ncov_v.at[pl.ds(0, NT)], lsem.at[2]),
        pltpu.make_async_copy(prior, prior_v, lsem.at[3]),
        pltpu.make_async_copy(small, small_v, lsem.at[4]),
        pltpu.make_async_copy(idft, idft_v, lsem.at[5]),
    ]
    for copy in locals_:
        copy.start()

    scope = jax.named_scope
    barrier = pltpu.get_barrier_semaphore()

    @pl.loop(1, NS)
    def _(k):
        pl.semaphore_signal(barrier, inc=1, device_id={"sens": lax.rem(me + k, NS)}, device_id_type=MESH)

    @pl.loop(1, NP)
    def _(k):
        pl.semaphore_signal(barrier, inc=1, device_id={"pts": lax.rem(mp + k, NP)}, device_id_type=MESH)

    with scope("entry_barrier"):
        pl.semaphore_wait(barrier, NS + NP - 2)

    at_z, at_x, at_core = me // 16, (me // 2) % 8, me % 2

    def partner(k):
        return ((at_z + k % 4) % 4) * 16 + ((at_x + (k // 4) % 8) % 8) * 2 + (at_core + k // 32) % 2

    def k_copy(peer):
        return pltpu.make_async_remote_copy(
            src_ref=kx.at[:, pl.ds(first_bin(chunk_of(peer)), FB)],
            dst_ref=raw.at[me],
            send_sem=ksend.at[peer],
            recv_sem=krecv.at[me],
            device_id={"sens": peer},
            device_id_type=MESH,
        )

    def k_arrived(peer):
        return pltpu.make_async_copy(kx.at[:, pl.ds(0, FB)], raw.at[peer], krecv.at[peer])

    def row_copy(src, dst, ss, rs, peer):
        return pltpu.make_async_remote_copy(
            src_ref=src.at[peer],
            dst_ref=dst.at[me],
            send_sem=ss.at[peer],
            recv_sem=rs.at[me],
            device_id={"sens": peer},
            device_id_type=MESH,
        )

    def row_arrived(src, dst, rs, peer):
        return pltpu.make_async_copy(src.at[peer], dst.at[peer], rs.at[peer])

    def start_k(k):
        peer = partner(k)

        @pl.when(is_owner(peer))
        def _():
            k_copy(peer).start()

    own = pltpu.make_async_copy(kx.at[:, pl.ds(first_bin(my_chunk), FB)], raw.at[me], krecv.at[me])

    @pl.when(mine)
    def _():
        own.start()

    with scope("send_spectra_first"):
        pl.loop(1, FIRST)(start_k)

    time = lax.broadcasted_iota(jnp.int32, (2, NT), 1)
    masks = [(time < wl[s]).astype(f32) for s in range(2)]
    start = [obs[s] * masks[s] for s in range(2)]

    def select(table_v):
        @pl.loop(0, TP // 16)
        def _(i):
            rows = pl.ds(pl.multiple_of(i * 16, 16), 16)
            block = table_v[rows].astype(f32)
            which = lax.broadcasted_iota(jnp.int32, block.shape, 1)
            for s in range(2):
                tsel[s, rows, :] = jnp.where(which == sb[s], block, 0.0).sum(axis=1).astype(bf16)

    def apply_selected(x):
        out = []
        for s in range(2):
            a, b, c = parts3(x[s])
            stacked = jnp.concatenate([a, b, c, jnp.zeros_like(a)], axis=0).astype(bf16)
            y = nt_dot(stacked, tsel[s])[:, :NT]
            out.append(masks[s] * (y[0:2] + y[2:4] + y[4:6]))
        return out

    with scope("direction"):
        locals_[0].wait()
        select(ninv_v)
        direction = apply_selected(start)

    with scope("spectrum"):
        locals_[1].wait()
        d4 = jnp.concatenate(direction, axis=0)
        da, db, dc = parts3(d4)
        d128 = jnp.concatenate([da] * 8 + [db] * 8 + [dc] * 8 + [jnp.zeros_like(da)] * 8, axis=0).astype(bf16)
        lane = lax.broadcasted_iota(jnp.int32, (NS, 128), 1)
        hat = jnp.zeros((NS, 128), f32)
        for part, table in enumerate(parts2(dft_v[...])):
            full = nt_dot(table, d128)
            picked = jnp.zeros((NS, 128), f32)
            for xf in range(8):
                picked += jnp.where((lane % 32) // 4 == xf, full[xf * NS : (xf + 1) * NS], 0.0)
            hat += picked + pltpu.roll(picked, 96, 1)
            if part == 0:
                hat += pltpu.roll(picked, 64, 1)
        hat = jnp.where(lane < 32, hat, 0.0)
        hsend[...] = hat.reshape(NS, 1, 128)

    with scope("send_spectrum_rows"):
        @pl.loop(1, NS)
        def _(k):
            peer = partner(k)

            @pl.when(is_owner(peer))
            def _():
                row_copy(hsend, hrecv, hss, hrs, peer).start()

    with scope("send_spectra_rest"):
        pl.loop(FIRST, NS)(start_k)
    hrecv[me] = hsend[me]

    with scope("covariance"):
        locals_[2].wait()
        select(ncov_v)
        cov = apply_selected(direction)
        inner = sum(jnp.sum(start[s] * direction[s], axis=1, keepdims=True) for s in range(2))
        curve = sum(jnp.sum(cov[s] * direction[s], axis=1, keepdims=True) for s in range(2))
        for copy in locals_[3:]:
            copy.wait()

        lane1 = lax.broadcasted_iota(jnp.int32, (1, 128), 1)
        known = jnp.zeros((1, 128), f32)
        for at, value in ((34, inner[0:1]), (35, inner[1:2]), (36, curve[0:1]), (37, curve[1:2])):
            known += jnp.where(lane1 == at, value, 0.0)

    with scope("bins"):
        @pl.when(mine)
        def _():
            @pl.loop(1, NS)
            def _(k):
                peer = partner(k)
                row_arrived(hsend, hrecv, hrs, peer).wait()

            rows = hrecv[...]
            twice = rows + pltpu.roll(rows.reshape(NS, 128), 32, 1).reshape(NS, 1, 128)
            z = (jnp.broadcast_to(twice, (NS, 16, 128)) * small_v[160:176, 0:128][None]).reshape(NS * 16, 128).astype(bf16)
            h = nt_dot(small_v[144:160, 0:128].astype(bf16), z).astype(bf16)

            with scope("wait_spectra"):

                @pl.loop(0, NS)
                def _(k):
                    peer = partner(k)
                    k_arrived(peer).wait()
                    kk[pl.ds(pl.multiple_of(peer * 16, 16), 16), :] = raw[peer].reshape(16, PD)

            adjoint = jnp.dot(h, kk[...], preferred_element_type=f32).astype(bf16)
            weighted = jnp.dot(adjoint, prior_v[...], preferred_element_type=f32).astype(bf16)
            spread = nt_dot(weighted, prior_v[...]).astype(bf16)
            spread = jnp.dot(small_v[176:304, 0:16].astype(bf16), spread, preferred_element_type=f32).astype(bf16)
            cross = nt_dot(kk[...], spread)
            folded = (cross.reshape(NS, 16, 128) * small_v[160:176, 0:128][None]).sum(axis=1)
            folded = folded + pltpu.roll(folded, 96, 1)
            folded = jnp.where(lane < 32, folded, 0.0)
            bins = first_bin(my_chunk) + (lane % 16) // 4
            weight = jnp.where((bins == 0) | (bins == NT // 2), 1.0, 2.0) / NT
            terms = folded * rows.reshape(NS, 128) * weight
            for r in range(2):
                value = jnp.sum(jnp.where(lane % 2 == r, terms, 0.0), keepdims=True)
                folded = folded + jnp.where(lane == 32 + r, value, 0.0)
            vsend[...] = (folded + known).reshape(NS, 1, 128)

    @pl.when(jnp.logical_not(mine))
    def _():
        vsend[...] = jnp.broadcast_to(known[None], (NS, 1, 128))

    with scope("send_forward_rows"):
        @pl.loop(1, NS)
        def _(k):
            row_copy(vsend, vrecv, vss, vrs, partner(k)).start()

    vrecv[me] = vsend[me]

    with scope("wait_spectra_sent"):

        @pl.loop(1, NS)
        def _(k):
            peer = partner(k)

            @pl.when(is_owner(peer))
            def _():
                k_copy(peer).wait_send()
                row_copy(hsend, hrecv, hss, hrs, peer).wait_send()

    with scope("wait_forward_rows"):

        @pl.loop(1, NS)
        def _(k):
            row_arrived(vsend, vrecv, vrs, partner(k)).wait()

    got = vrecv[...].reshape(NS, 128)
    total = jnp.sum(got, axis=0, keepdims=True)
    got = jnp.where(lane < 32, got, 0.0)
    packed = got[0:16]
    for q in range(1, 4):
        packed += pltpu.roll(got[16 * q : 16 * q + 16], 32 * q, 1)
    row16 = lax.broadcasted_iota(jnp.int32, (16, 128), 0)
    lane16 = lax.broadcasted_iota(jnp.int32, (16, 128), 1)
    spare = jnp.broadcast_to(pltpu.roll(jnp.where((lane1 == 32) | (lane1 == 33), total, 0.0), 64, 1), (16, 128))
    packed = jnp.where((row16 == 15) & (lane16 >= 96), spare, packed)
    psend[...] = packed
    precv[mp] = packed

    def p_copy(peer):
        return pltpu.make_async_remote_copy(
            src_ref=psend,
            dst_ref=precv.at[mp],
            send_sem=pss.at[peer],
            recv_sem=prs.at[mp],
            device_id={"pts": peer},
            device_id_type=MESH,
        )

    def p_arrived(peer):
        return pltpu.make_async_copy(psend, precv.at[peer], prs.at[peer])

    with scope("send_over_pts"):

        @pl.loop(1, NP)
        def _(k):
            p_copy(lax.rem(mp + k, NP)).start()

    with scope("wait_forward_sent"):

        @pl.loop(1, NS)
        def _(k):
            row_copy(vsend, vrecv, vss, vrs, partner(k)).wait_send()

    with scope("wait_over_pts"):

        @pl.loop(1, NP)
        def _(k):
            p_arrived(lax.rem(mp + k, NP)).wait()

    forward = jnp.sum(precv[...], axis=0)

    def at_lane(x, n):
        return jnp.sum(jnp.where(lax.broadcasted_iota(jnp.int32, x.shape, 1) == n, x, 0.0), axis=1, keepdims=True)

    last = forward[15:16]
    step = [at_lane(total, 34 + r) / (at_lane(last, 96 + r) + at_lane(total, 36 + r)) for r in range(2)]
    fa = forward.astype(bf16)
    fb = (forward - fa.astype(f32)).astype(bf16)
    spread_out = []
    for part in (fa, fb):
        tiled = lax.dot_general(part, small_v[128:144].astype(bf16), (((0,), (0,)), ((), ())), preferred_element_type=f32)
        tiled = (tiled * small_v[0:128]).astype(bf16)
        spread_out.append(jnp.dot(small_v[304:312, 0:128].astype(bf16), tiled, preferred_element_type=f32)[0:4])
    both = jnp.concatenate(spread_out, axis=0).astype(bf16)
    hi, lo = (jnp.dot(both, table, preferred_element_type=f32) for table in parts2(idft_v[...]))
    signal = hi[0:4] + hi[4:8] + lo[0:4]
    row2 = lax.broadcasted_iota(jnp.int32, (2, NT), 0)
    size = jnp.where(row2 == 0, step[0], step[1])
    for s in range(2):
        image = cov[s] + masks[s] * signal[2 * s : 2 * s + 2]
        sol[s] = size * direction[s]
        res[s] = start[s] - size * image

    @pl.loop(1, NP)
    def _(k):
        p_copy(lax.rem(mp + k, NP)).wait_send()


def shards(observed, spectra, prior_factor, noise_cov, noise_inv, sensor_block, window_len):
    vmem, smem, any_ = (pl.BlockSpec(memory_space=m) for m in (pltpu.VMEM, pltpu.SMEM, pl.ANY))
    dma = pltpu.SemaphoreType.DMA
    out = jax.ShapeDtypeStruct((2, 2, NT), f32)
    return pl.pallas_call(
        kernel,
        out_shape=(out, out),
        in_specs=[smem, smem, vmem] + [any_] * 7,
        out_specs=(vmem, vmem),
        scratch_shapes=[
            pltpu.VMEM((NS, 2, FB, 2, PD), bf16),
            pltpu.VMEM((NS * 16, PD), bf16),
            pltpu.VMEM((PD, PD), bf16),
            pltpu.VMEM((TP, NB, NT), bf16),
            pltpu.VMEM((TP, NB, NT), bf16),
            pltpu.VMEM((512, NT), f32),
            pltpu.VMEM((512, NT), f32),
            pltpu.VMEM((2, TP, NT), bf16),
            pltpu.VMEM((NS, 1, 128), f32),
            pltpu.VMEM((NS, 1, 128), f32),
            pltpu.VMEM((NS, 1, 128), f32),
            pltpu.VMEM((NS, 1, 128), f32),
            pltpu.VMEM((16, 128), f32),
            pltpu.VMEM((NP, 16, 128), f32),
            pltpu.VMEM((312, 512), f32),
            dma((6,)),
            dma((NS,)), dma((NS,)), dma((NS,)), dma((NS,)), dma((NS,)), dma((NS,)),
            dma((NP,)), dma((NP,)),
        ],
        compiler_params=pltpu.CompilerParams(
            collective_id=0, has_side_effects=True, vmem_limit_bytes=60 << 20
        ),
        cost_estimate=pl.CostEstimate(flops=10**10, bytes_accessed=10**7, transcendentals=0),
    )(
        window_len, sensor_block, observed, spectra, prior_factor,
        noise_inv.transpose(1, 0, 2), noise_cov.transpose(1, 0, 2),
        *tables(),
    )


def solution(mesh):
    placed = (
        P("sens", None, None),
        P(None, None, "sens", "pts"),
        P("pts", None),
        P(),
        P(),
        P("sens"),
        P("sens"),
    )
    return jax.shard_map(
        shards,
        mesh=mesh,
        in_specs=placed,
        out_specs=(P("sens", None, None), P("sens", None, None)),
        check_vma=False,
    )
```

```python
import functools
import math

import jax
import jax.numpy as jnp
import numpy as np
from jax import lax
from jax.experimental import pallas as pl
from jax.experimental.pallas import tpu as pltpu
from jax.sharding import PartitionSpec as P

MESH = pl.DeviceIdType.MESH
NT, F, PD, NB = 420, 211, 768, 4
NS, NP = 64, 16
FB = 4
NC = -(-F // FB)
TP = 432
f32, bf16 = jnp.float32, jnp.bfloat16


def chunk_of(dev):
    return (dev * NC + NS - 1) // NS


def first_bin(c):
    return jnp.minimum(FB * c, F - FB)


def is_owner(dev):
    return chunk_of(dev + 1) != chunk_of(dev)


@functools.cache
def tables():
    t = np.arange(NT)
    fwd = np.zeros((2, FB, NS, NT))
    inv = np.zeros((NS, 2, FB, NT))
    for dev in range(NS):
        c = -(-dev * NC // NS)
        if (c * NS) // NC != dev or c >= NC:
            continue
        for f in range(FB):
            bin_ = min(FB * c, F - FB) + f
            if bin_ < FB * c:
                continue
            phase = (t * bin_) % NT
            cosine = np.cos(2 * math.pi * phase / NT)
            sine = np.where(phase % (NT // 2) == 0, 0.0, np.sin(2 * math.pi * phase / NT))
            weight = (1.0 if bin_ in (0, NT // 2) else 2.0) / NT
            fwd[0, f, dev], fwd[1, f, dev] = cosine, -sine
            inv[dev, 0, f], inv[dev, 1, f] = cosine * weight, -sine * weight
    fwd = fwd.reshape(2 * FB * NS, NT)
    inv = inv.reshape(4, 16, 8, NT).transpose(0, 2, 1, 3).reshape(512, NT)
    gt = np.zeros((128, 16))
    mask = np.zeros((16, 128))
    for xk in range(2):
        for x in range(2):
            for f in range(FB):
                for s in range(2):
                    mask[xk * 8 + f * 2 + s, xk * 32 + x * 16 + f * 4 + s * 2 :][:2] = 1
                    for r in range(2):
                        m = xk * 32 + x * 16 + f * 4 + s * 2 + r
                        j = f * 4 + (x if xk == 0 else 1 - x) * 2 + r
                        gt[m, j] = 1 if xk == 0 or x == 1 else -1
    rep = np.tile(np.eye(16), (1, 32))
    pick = np.zeros((128, 512))
    for row in range(128):
        pick[row, (row // 4) * 16 : (row // 4) * 16 + 16] = 1
    fold = np.zeros((8, 128))
    for row in range(128):
        fold[row % 4, row] = 1
    small = np.zeros((312, 512))
    small[0:128] = pick
    small[128:144] = rep
    small[144:160, :128] = gt.T
    small[160:176, :128] = mask
    small[176:304, :16] = gt
    small[304:312, :128] = fold
    return [a.astype(np.float32) for a in (fwd, inv, small)]


def parts3(x):
    a = x.astype(bf16).astype(f32)
    b = (x - a).astype(bf16).astype(f32)
    return a, b, x - a - b


def parts2(x):
    a = x.astype(bf16)
    return a, (x - a.astype(f32)).astype(bf16)


def nt_dot(a, b):
    return lax.dot_general(a, b, (((1,), (1,)), ((), ())), preferred_element_type=f32)


def kernel(
    wl_any, sb_any, obs_any, kx, prior, ninv, ncov, dft, idft, small,
    out,
    wl, sb, obs, raw, kk, prior_v, ninv_v, ncov_v, dft_v, idft_v, idft_2, tsel, hsend, hrecv, vsend, vrecv, psend, precv, small_v,
    lsem, krecv, ksend, hss, hrs, vss, vrs, pss, prs,
):
    me, mp = lax.axis_index("sens"), lax.axis_index("pts")
    mine = is_owner(me)
    my_chunk = chunk_of(me)
    at_x, in_z, in_core = (me // 2) % 8, me // 16, me % 2
    at_z = [((in_z + dz) % 4) * 16 for dz in range(4)]
    at_core = [in_core, 1 - in_core]

    def partners(body, low=0, high=4):
        @pl.loop(low, high)
        def _(t):
            for back_x in range(2):
                step = t if back_x == 0 else jnp.where(t == 0, 4, 8 - t)
                x = ((at_x + step) % 8) * 2
                there = jnp.where(t == 0, back_x, 1 - back_x) * 8 + t * 16
                for dz in range(4):
                    for dc in range(2):
                        todo = functools.partial(
                            body,
                            at_z[dz] + x + at_core[dc],
                            t * 16 + back_x * 8 + dz * 2 + dc,
                            there + (-dz % 4) * 2 + dc,
                            t,
                        )
                        if back_x == dz == dc == 0:
                            pl.when(t != 0)(todo)
                        else:
                            todo()

    def others(body):
        for k in range(1, NP):
            body((mp + k) % NP)

    barrier = pltpu.get_barrier_semaphore()
    partners(
        lambda peer, *_: pl.semaphore_signal(barrier, inc=1, device_id={"sens": peer}, device_id_type=MESH)
    )
    others(lambda peer: pl.semaphore_signal(barrier, inc=1, device_id={"pts": peer}, device_id_type=MESH))

    locals_ = [
        pltpu.make_async_copy(wl_any, wl, lsem.at[0]),
        pltpu.make_async_copy(sb_any, sb, lsem.at[1]),
        pltpu.make_async_copy(obs_any, obs, lsem.at[2]),
        pltpu.make_async_copy(ninv, ninv_v.at[pl.ds(0, NT)], lsem.at[3]),
        pltpu.make_async_copy(dft, dft_v, lsem.at[4]),
        pltpu.make_async_copy(ncov, ncov_v.at[pl.ds(0, NT)], lsem.at[5]),
        pltpu.make_async_copy(prior, prior_v, lsem.at[6]),
        pltpu.make_async_copy(small, small_v, lsem.at[7]),
        pltpu.make_async_copy(idft, idft_v, lsem.at[8]),
    ]
    for copy in locals_:
        copy.start()
    own = pltpu.make_async_copy(kx.at[:, pl.ds(first_bin(jnp.minimum(my_chunk, NC - 1)), FB)], raw.at[0], krecv.at[0])

    @pl.when(mine)
    def _():
        own.start()

    pl.semaphore_wait(barrier, NS + NP - 2)

    def remote(src, dst, send, recv, peer):
        return pltpu.make_async_remote_copy(
            src_ref=src, dst_ref=dst, send_sem=send, recv_sem=recv, device_id=peer, device_id_type=MESH
        )

    def finish(like, sem):
        pltpu.make_async_copy(like, like, sem).wait()

    def send_bins(peer, slot, there, t):
        @pl.when(is_owner(peer))
        def _():
            first = first_bin(chunk_of(peer))
            remote(kx.at[:, pl.ds(first, FB)], raw.at[there], ksend, krecv.at[t], {"sens": peer}).start()

    partners(send_bins, 0, 3)

    for copy in locals_[:4]:
        copy.wait()

    time = lax.broadcasted_iota(jnp.int32, (2, NT), 1)
    masks = [(time < wl[s]).astype(f32) for s in range(2)]
    start = [obs[s] * masks[s] for s in range(2)]

    def select(table_v):
        @pl.loop(0, TP // 16)
        def _(i):
            rows = pl.ds(pl.multiple_of(i * 16, 16), 16)
            block = table_v[rows].astype(f32)
            which = lax.broadcasted_iota(jnp.int32, block.shape, 1)
            for s in range(2):
                tsel[s, rows, :] = jnp.where(which == sb[s], block, 0.0).sum(axis=1).astype(bf16)

    def apply_selected(x):
        out = []
        for s in range(2):
            a, b, c = parts3(x[s])
            stacked = jnp.concatenate([a, b, c, jnp.zeros_like(a)], axis=0).astype(bf16)
            y = nt_dot(stacked, tsel[s])[:, :NT]
            out.append(masks[s] * (y[0:2] + y[2:4] + y[4:6]))
        return out

    select(ninv_v)
    direction = apply_selected(start)

    locals_[4].wait()
    d4 = jnp.concatenate(direction, axis=0)
    da, db, dc = parts3(d4)
    d128 = jnp.concatenate([da] * 8 + [db] * 8 + [dc] * 8 + [jnp.zeros_like(da)] * 8, axis=0).astype(bf16)
    lane = lax.broadcasted_iota(jnp.int32, (NS, 128), 1)
    hat = jnp.zeros((NS, 128), f32)
    for part, table in enumerate(parts2(dft_v[...])):
        full = nt_dot(table, d128)
        picked = jnp.zeros((NS, 128), f32)
        for xf in range(8):
            picked += jnp.where((lane % 32) // 4 == xf, full[xf * NS : (xf + 1) * NS], 0.0)
        hat += picked + pltpu.roll(picked, 96, 1)
        if part == 0:
            hat += pltpu.roll(picked, 64, 1)
    hat = jnp.where(lane < 32, hat, 0.0)
    hsend[...] = hat.reshape(NS, 1, 128)

    def send_hat(peer, slot, there, t):
        @pl.when(is_owner(peer))
        def _():
            remote(hsend.at[peer], hrecv.at[there], hss, hrs, {"sens": peer}).start()

    partners(send_hat)
    partners(send_bins, 3, 4)
    hrecv[0] = hsend[me]

    locals_[5].wait()
    select(ncov_v)
    cov = apply_selected(direction)
    inner = sum(jnp.sum(start[s] * direction[s], axis=1, keepdims=True) for s in range(2))
    curve = sum(jnp.sum(cov[s] * direction[s], axis=1, keepdims=True) for s in range(2))
    for copy in locals_[6:]:
        copy.wait()
    idft_2[0], idft_2[1] = parts2(idft_v[...])

    lane1 = lax.broadcasted_iota(jnp.int32, (1, 128), 1)
    known = jnp.zeros((1, 128), f32)
    for at, value in ((34, inner[0:1]), (35, inner[1:2]), (36, curve[0:1]), (37, curve[1:2])):
        known += jnp.where(lane1 == at, value, 0.0)
    mask16 = small_v[160:176, 0:128]

    @pl.when(mine)
    def _():
        finish(hrecv.at[pl.ds(0, NS - 1)], hrs)
        rows = hrecv[...]
        twice = rows + pltpu.roll(rows.reshape(NS, 128), 32, 1).reshape(NS, 1, 128)
        z = (jnp.broadcast_to(twice, (NS, 16, 128)) * mask16[None]).reshape(NS * 16, 128).astype(bf16)
        h = nt_dot(small_v[144:160, 0:128].astype(bf16), z).astype(bf16)

        @pl.loop(0, 4)
        def _(t):
            finish(raw.at[pl.ds(t * 16, 16)], krecv.at[t])

            @pl.loop(0, 16)
            def _(i):
                slot = t * 16 + i
                kk[pl.ds(pl.multiple_of(slot * 16, 16), 16), :] = raw[slot].reshape(16, PD)

        adjoint = jnp.dot(h, kk[...], preferred_element_type=f32).astype(bf16)
        weighted = jnp.dot(adjoint, prior_v[...], preferred_element_type=f32).astype(bf16)
        spread = nt_dot(weighted, prior_v[...]).astype(bf16)
        spread = jnp.dot(small_v[176:304, 0:16].astype(bf16), spread, preferred_element_type=f32).astype(bf16)
        cross = nt_dot(kk[...], spread)
        folded = (cross.reshape(NS, 16, 128) * mask16[None]).sum(axis=1)
        folded = folded + pltpu.roll(folded, 96, 1)
        folded = jnp.where(lane < 32, folded, 0.0)
        bins = first_bin(my_chunk) + (lane % 16) // 4
        weight = jnp.where((bins == 0) | (bins == NT // 2), 1.0, 2.0) / NT
        terms = folded * rows.reshape(NS, 128) * weight
        for r in range(2):
            value = jnp.sum(jnp.where(lane % 2 == r, terms, 0.0), keepdims=True)
            folded = folded + jnp.where(lane == 32 + r, value, 0.0)
        vsend[...] = (folded + known).reshape(NS, 1, 128)

    @pl.when(jnp.logical_not(mine))
    def _():
        vsend[...] = jnp.broadcast_to(known[None], (NS, 1, 128))

    partners(lambda peer, slot, there, t: remote(vsend.at[slot], vrecv.at[me], vss, vrs, {"sens": peer}).start())
    vrecv[me] = vsend[0]

    for is_mine, count in ((mine, NC - 1), (jnp.logical_not(mine), NC)):

        @pl.when(is_mine)
        def _():
            finish(raw.at[pl.ds(0, count)], ksend)
            finish(hsend.at[pl.ds(0, count)], hss)

    finish(vrecv.at[pl.ds(0, NS - 1)], vrs)

    got = vrecv[...].reshape(NS, 128)
    total = jnp.sum(got, axis=0, keepdims=True)
    got = jnp.where(lane < 32, got, 0.0)
    packed = got[0:16]
    for q in range(1, 4):
        packed += pltpu.roll(got[16 * q : 16 * q + 16], 32 * q, 1)
    row16 = lax.broadcasted_iota(jnp.int32, (16, 128), 0)
    lane16 = lax.broadcasted_iota(jnp.int32, (16, 128), 1)
    spare = jnp.broadcast_to(pltpu.roll(jnp.where((lane1 == 32) | (lane1 == 33), total, 0.0), 64, 1), (16, 128))
    packed = jnp.where((row16 == 15) & (lane16 >= 96), spare, packed)
    psend[...] = packed
    others(lambda peer: remote(psend, precv.at[mp], pss, prs, {"pts": peer}).start())
    precv[mp] = packed
    finish(vsend.at[pl.ds(0, NS - 1)], vss)
    finish(precv.at[pl.ds(0, NP - 1)], prs)
    forward = jnp.sum(precv[...], axis=0)

    def at_lane(x, n):
        return jnp.sum(jnp.where(lax.broadcasted_iota(jnp.int32, x.shape, 1) == n, x, 0.0), axis=1, keepdims=True)

    last = forward[15:16]
    step = [at_lane(total, 34 + r) / (at_lane(last, 96 + r) + at_lane(total, 36 + r)) for r in range(2)]
    spread_out = []
    for part in parts2(forward):
        tiled = lax.dot_general(part, small_v[128:144].astype(bf16), (((0,), (0,)), ((), ())), preferred_element_type=f32)
        tiled = (tiled * small_v[0:128]).astype(bf16)
        spread_out.append(jnp.dot(small_v[304:312, 0:128].astype(bf16), tiled, preferred_element_type=f32)[0:4])
    both = jnp.concatenate(spread_out, axis=0).astype(bf16)
    hi, lo = (jnp.dot(both, idft_2[part], preferred_element_type=f32) for part in range(2))
    signal = hi[0:4] + hi[4:8] + lo[0:4]
    row2 = lax.broadcasted_iota(jnp.int32, (2, NT), 0)
    size = jnp.where(row2 == 0, step[0], step[1])
    for s in range(2):
        image = cov[s] + masks[s] * signal[2 * s : 2 * s + 2]
        out[0, s] = size * direction[s]
        out[1, s] = start[s] - size * image
    finish(precv.at[pl.ds(0, NP - 1)], pss)


def shards(observed, spectra, prior_factor, noise_cov, noise_inv, sensor_block, window_len):
    any_ = pl.BlockSpec(memory_space=pl.ANY)
    dma, vmem = pltpu.SemaphoreType.DMA, pltpu.VMEM
    both = pl.pallas_call(
        kernel,
        out_shape=jax.ShapeDtypeStruct((2, 2, 2, NT), f32),
        in_specs=[any_] * 10,
        out_specs=pl.BlockSpec(memory_space=vmem),
        scratch_shapes=[
            pltpu.SMEM((2,), jnp.int32),
            pltpu.SMEM((2,), jnp.int32),
            vmem((2, 2, NT), f32),
            vmem((NS, 2, FB, 2, PD), bf16),
            vmem((NS * 16, PD), bf16),
            vmem((PD, PD), bf16),
            vmem((TP, NB, NT), bf16),
            vmem((TP, NB, NT), bf16),
            vmem((512, NT), f32),
            vmem((512, NT), f32),
            vmem((2, 512, NT), bf16),
            vmem((2, TP, NT), bf16),
            vmem((NS, 1, 128), f32),
            vmem((NS, 1, 128), f32),
            vmem((NS, 1, 128), f32),
            vmem((NS, 1, 128), f32),
            vmem((16, 128), f32),
            vmem((NP, 16, 128), f32),
            vmem((312, 512), f32),
            dma((9,)),
            dma((4,)),
        ]
        + [dma(())] * 7,
        compiler_params=pltpu.CompilerParams(
            collective_id=0, has_side_effects=True, vmem_limit_bytes=60 << 20
        ),
        cost_estimate=pl.CostEstimate(flops=10**10, bytes_accessed=10**7, transcendentals=0),
    )(
        window_len, sensor_block, observed, spectra, prior_factor,
        noise_inv.transpose(1, 0, 2), noise_cov.transpose(1, 0, 2),
        *tables(),
    )
    return both[0], both[1]


def solution(mesh):
    placed = (
        P("sens", None, None),
        P(None, None, "sens", "pts"),
        P("pts", None),
        P(),
        P(),
        P("sens"),
        P("sens"),
    )
    return jax.shard_map(
        shards,
        mesh=mesh,
        in_specs=placed,
        out_specs=(P("sens", None, None), P("sens", None, None)),
        check_vma=False,
    )
```

```python
import functools
import math

import jax
import jax.numpy as jnp
import numpy as np
from jax import lax
from jax.experimental import pallas as pl
from jax.experimental.pallas import tpu as pltpu
from jax.sharding import PartitionSpec as P

MESH = pl.DeviceIdType.MESH
NT, F, PD, NB = 420, 211, 768, 4
NS, NP = 64, 16
FB = 4
NC = -(-F // FB)
TP = 432
f32, bf16 = jnp.float32, jnp.bfloat16


def chunk_of(dev):
    return (dev * NC + NS - 1) // NS


def first_bin(c):
    return jnp.minimum(FB * c, F - FB)


def is_owner(dev):
    return chunk_of(dev + 1) != chunk_of(dev)


@functools.cache
def tables():
    t = np.arange(NT)
    fwd = np.zeros((2, FB, NS, NT))
    inv = np.zeros((NS, 2, FB, NT))
    for dev in range(NS):
        c = -(-dev * NC // NS)
        if (c * NS) // NC != dev or c >= NC:
            continue
        for f in range(FB):
            bin_ = min(FB * c, F - FB) + f
            if bin_ < FB * c:
                continue
            phase = (t * bin_) % NT
            cosine = np.cos(2 * math.pi * phase / NT)
            sine = np.where(phase % (NT // 2) == 0, 0.0, np.sin(2 * math.pi * phase / NT))
            weight = (1.0 if bin_ in (0, NT // 2) else 2.0) / NT
            fwd[0, f, dev], fwd[1, f, dev] = cosine, -sine
            inv[dev, 0, f], inv[dev, 1, f] = cosine * weight, -sine * weight
    fwd = fwd.reshape(2 * FB * NS, NT)
    inv = inv.reshape(4, 16, 8, NT).transpose(0, 2, 1, 3).reshape(512, NT)
    gt = np.zeros((128, 16))
    mask = np.zeros((16, 128))
    for xk in range(2):
        for x in range(2):
            for f in range(FB):
                for s in range(2):
                    mask[xk * 8 + f * 2 + s, xk * 32 + x * 16 + f * 4 + s * 2 :][:2] = 1
                    for r in range(2):
                        m = xk * 32 + x * 16 + f * 4 + s * 2 + r
                        j = f * 4 + (x if xk == 0 else 1 - x) * 2 + r
                        gt[m, j] = 1 if xk == 0 or x == 1 else -1
    rep = np.tile(np.eye(16), (1, 32))
    pick = np.zeros((128, 512))
    for row in range(128):
        pick[row, (row // 4) * 16 : (row // 4) * 16 + 16] = 1
    fold = np.zeros((8, 128))
    for row in range(128):
        fold[row % 4, row] = 1
    small = np.zeros((312, 512))
    small[0:128] = pick
    small[128:144] = rep
    small[144:160, :128] = gt.T
    small[160:176, :128] = mask
    small[176:304, :16] = gt
    small[304:312, :128] = fold
    return [a.astype(np.float32) for a in (fwd, inv, small)]


def parts3(x):
    a = x.astype(bf16).astype(f32)
    b = (x - a).astype(bf16).astype(f32)
    return a, b, x - a - b


def parts2(x):
    a = x.astype(bf16)
    return a, (x - a.astype(f32)).astype(bf16)


def nt_dot(a, b):
    return lax.dot_general(a, b, (((1,), (1,)), ((), ())), preferred_element_type=f32)


def kernel(
    wl_any, sb_any, obs_any, kx, prior, ninv, ncov, dft, idft, small,
    out,
    wl, sb, obs, raw, kk, prior_v, ninv_v, ncov_v, dft_v, idft_v, idft_2, tsel, hsend, hrecv, vsend, vrecv, psend, precv, small_v,
    lsem, krecv, ksend, hss, hrs, vss, vrs, pss, prs,
):
    me, mp = lax.axis_index("sens"), lax.axis_index("pts")
    mine = is_owner(me)
    my_chunk = chunk_of(me)
    at_x, in_z, in_core = (me // 2) % 8, me // 16, me % 2
    at_z = [((in_z + dz) % 4) * 16 for dz in range(4)]

    def partners(body, low=0, high=16):
        @pl.loop(low, high)
        def _(u):
            dc, dx = u // 8, u % 8
            base = ((at_x + dx) % 8) * 2 + (in_core + dc) % 2
            here = dc * 32 + ((8 - dx) % 8) * 4
            for dz in range(4):
                todo = functools.partial(body, at_z[dz] + base, here + -dz % 4, u * 4 + dz, u // 4)
                if dz == 0:
                    pl.when(u != 0)(todo)
                else:
                    todo()

    def others(body):
        for k in range(1, NP):
            body((mp + k) % NP)

    barrier = pltpu.get_barrier_semaphore()
    partners(
        lambda peer, *_: pl.semaphore_signal(barrier, inc=1, device_id={"sens": peer}, device_id_type=MESH)
    )
    others(lambda peer: pl.semaphore_signal(barrier, inc=1, device_id={"pts": peer}, device_id_type=MESH))

    locals_ = [
        pltpu.make_async_copy(wl_any, wl, lsem.at[0]),
        pltpu.make_async_copy(sb_any, sb, lsem.at[1]),
        pltpu.make_async_copy(obs_any, obs, lsem.at[2]),
        pltpu.make_async_copy(ninv, ninv_v.at[pl.ds(0, NT)], lsem.at[3]),
        pltpu.make_async_copy(dft, dft_v, lsem.at[4]),
        pltpu.make_async_copy(ncov, ncov_v.at[pl.ds(0, NT)], lsem.at[5]),
        pltpu.make_async_copy(prior, prior_v, lsem.at[6]),
        pltpu.make_async_copy(small, small_v, lsem.at[7]),
        pltpu.make_async_copy(idft, idft_v, lsem.at[8]),
    ]
    for copy in locals_:
        copy.start()
    own = pltpu.make_async_copy(kx.at[:, pl.ds(first_bin(jnp.minimum(my_chunk, NC - 1)), FB)], raw.at[0], krecv.at[0])

    @pl.when(mine)
    def _():
        own.start()

    pl.semaphore_wait(barrier, NS + NP - 2)

    def remote(src, dst, send, recv, peer):
        return pltpu.make_async_remote_copy(
            src_ref=src, dst_ref=dst, send_sem=send, recv_sem=recv, device_id=peer, device_id_type=MESH
        )

    def finish(like, sem):
        pltpu.make_async_copy(like, like, sem).wait()

    def send_bins(peer, slot, there, t):
        @pl.when(is_owner(peer))
        def _():
            first = first_bin(chunk_of(peer))
            remote(kx.at[:, pl.ds(first, FB)], raw.at[there], ksend, krecv.at[t], {"sens": peer}).start()

    partners(send_bins, 0, 10)

    for copy in locals_[:4]:
        copy.wait()

    time = lax.broadcasted_iota(jnp.int32, (2, NT), 1)
    masks = [(time < wl[s]).astype(f32) for s in range(2)]
    start = [obs[s] * masks[s] for s in range(2)]

    def select(table_v):
        @pl.loop(0, TP // 16)
        def _(i):
            rows = pl.ds(pl.multiple_of(i * 16, 16), 16)
            block = table_v[rows].astype(f32)
            which = lax.broadcasted_iota(jnp.int32, block.shape, 1)
            for s in range(2):
                tsel[s, rows, :] = jnp.where(which == sb[s], block, 0.0).sum(axis=1).astype(bf16)

    def apply_selected(x):
        out = []
        for s in range(2):
            a, b, c = parts3(x[s])
            stacked = jnp.concatenate([a, b, c, jnp.zeros_like(a)], axis=0).astype(bf16)
            y = nt_dot(stacked, tsel[s])[:, :NT]
            out.append(masks[s] * (y[0:2] + y[2:4] + y[4:6]))
        return out

    select(ninv_v)
    direction = apply_selected(start)

    locals_[4].wait()
    d4 = jnp.concatenate(direction, axis=0)
    da, db, dc = parts3(d4)
    d128 = jnp.concatenate([da] * 8 + [db] * 8 + [dc] * 8 + [jnp.zeros_like(da)] * 8, axis=0).astype(bf16)
    lane = lax.broadcasted_iota(jnp.int32, (NS, 128), 1)
    hat = jnp.zeros((NS, 128), f32)
    for part, table in enumerate(parts2(dft_v[...])):
        full = nt_dot(table, d128)
        picked = jnp.zeros((NS, 128), f32)
        for xf in range(8):
            picked += jnp.where((lane % 32) // 4 == xf, full[xf * NS : (xf + 1) * NS], 0.0)
        hat += picked + pltpu.roll(picked, 96, 1)
        if part == 0:
            hat += pltpu.roll(picked, 64, 1)
    hat = jnp.where(lane < 32, hat, 0.0)
    hsend[...] = hat.reshape(NS, 1, 128)

    def send_hat(peer, slot, there, t):
        @pl.when(is_owner(peer))
        def _():
            remote(hsend.at[peer], hrecv.at[there], hss, hrs, {"sens": peer}).start()

    partners(send_hat)
    partners(send_bins, 10, 16)
    hrecv[0] = hsend[me]

    locals_[5].wait()
    select(ncov_v)
    cov = apply_selected(direction)
    inner = sum(jnp.sum(start[s] * direction[s], axis=1, keepdims=True) for s in range(2))
    curve = sum(jnp.sum(cov[s] * direction[s], axis=1, keepdims=True) for s in range(2))
    for copy in locals_[6:]:
        copy.wait()
    idft_2[0], idft_2[1] = parts2(idft_v[...])

    lane1 = lax.broadcasted_iota(jnp.int32, (1, 128), 1)
    known = jnp.zeros((1, 128), f32)
    for at, value in ((34, inner[0:1]), (35, inner[1:2]), (36, curve[0:1]), (37, curve[1:2])):
        known += jnp.where(lane1 == at, value, 0.0)
    mask16 = small_v[160:176, 0:128]

    @pl.when(mine)
    def _():
        finish(hrecv.at[pl.ds(0, NS - 1)], hrs)
        rows = hrecv[...]
        twice = rows + pltpu.roll(rows.reshape(NS, 128), 32, 1).reshape(NS, 1, 128)
        z = (jnp.broadcast_to(twice, (NS, 16, 128)) * mask16[None]).reshape(NS * 16, 128).astype(bf16)
        h = nt_dot(small_v[144:160, 0:128].astype(bf16), z).astype(bf16)

        @pl.loop(0, 4)
        def _(t):
            finish(raw.at[pl.ds(t * 16, 16)], krecv.at[t])

            @pl.loop(0, 16)
            def _(i):
                slot = t * 16 + i
                kk[pl.ds(pl.multiple_of(slot * 16, 16), 16), :] = raw[slot].reshape(16, PD)

        adjoint = jnp.dot(h, kk[...], preferred_element_type=f32).astype(bf16)
        weighted = jnp.dot(adjoint, prior_v[...], preferred_element_type=f32).astype(bf16)
        spread = nt_dot(weighted, prior_v[...]).astype(bf16)
        spread = jnp.dot(small_v[176:304, 0:16].astype(bf16), spread, preferred_element_type=f32).astype(bf16)
        cross = nt_dot(kk[...], spread)
        folded = (cross.reshape(NS, 16, 128) * mask16[None]).sum(axis=1)
        folded = folded + pltpu.roll(folded, 96, 1)
        folded = jnp.where(lane < 32, folded, 0.0)
        bins = first_bin(my_chunk) + (lane % 16) // 4
        weight = jnp.where((bins == 0) | (bins == NT // 2), 1.0, 2.0) / NT
        terms = folded * rows.reshape(NS, 128) * weight
        for r in range(2):
            value = jnp.sum(jnp.where(lane % 2 == r, terms, 0.0), keepdims=True)
            folded = folded + jnp.where(lane == 32 + r, value, 0.0)
        vsend[...] = (folded + known).reshape(NS, 1, 128)

    @pl.when(jnp.logical_not(mine))
    def _():
        vsend[...] = jnp.broadcast_to(known[None], (NS, 1, 128))

    partners(lambda peer, slot, there, t: remote(vsend.at[slot], vrecv.at[me], vss, vrs, {"sens": peer}).start())
    vrecv[me] = vsend[0]

    for is_mine, count in ((mine, NC - 1), (jnp.logical_not(mine), NC)):

        @pl.when(is_mine)
        def _():
            finish(raw.at[pl.ds(0, count)], ksend)
            finish(hsend.at[pl.ds(0, count)], hss)

    finish(vrecv.at[pl.ds(0, NS - 1)], vrs)

    got = vrecv[...].reshape(NS, 128)
    total = jnp.sum(got, axis=0, keepdims=True)
    got = jnp.where(lane < 32, got, 0.0)
    packed = got[0:16]
    for q in range(1, 4):
        packed += pltpu.roll(got[16 * q : 16 * q + 16], 32 * q, 1)
    row16 = lax.broadcasted_iota(jnp.int32, (16, 128), 0)
    lane16 = lax.broadcasted_iota(jnp.int32, (16, 128), 1)
    spare = jnp.broadcast_to(pltpu.roll(jnp.where((lane1 == 32) | (lane1 == 33), total, 0.0), 64, 1), (16, 128))
    packed = jnp.where((row16 == 15) & (lane16 >= 96), spare, packed)
    psend[...] = packed
    others(lambda peer: remote(psend, precv.at[mp], pss, prs, {"pts": peer}).start())
    precv[mp] = packed
    finish(vsend.at[pl.ds(0, NS - 1)], vss)
    finish(precv.at[pl.ds(0, NP - 1)], prs)
    forward = jnp.sum(precv[...], axis=0)

    def at_lane(x, n):
        return jnp.sum(jnp.where(lax.broadcasted_iota(jnp.int32, x.shape, 1) == n, x, 0.0), axis=1, keepdims=True)

    last = forward[15:16]
    step = [at_lane(total, 34 + r) / (at_lane(last, 96 + r) + at_lane(total, 36 + r)) for r in range(2)]
    spread_out = []
    for part in parts2(forward):
        tiled = lax.dot_general(part, small_v[128:144].astype(bf16), (((0,), (0,)), ((), ())), preferred_element_type=f32)
        tiled = (tiled * small_v[0:128]).astype(bf16)
        spread_out.append(jnp.dot(small_v[304:312, 0:128].astype(bf16), tiled, preferred_element_type=f32)[0:4])
    both = jnp.concatenate(spread_out, axis=0).astype(bf16)
    hi, lo = (jnp.dot(both, idft_2[part], preferred_element_type=f32) for part in range(2))
    signal = hi[0:4] + hi[4:8] + lo[0:4]
    row2 = lax.broadcasted_iota(jnp.int32, (2, NT), 0)
    size = jnp.where(row2 == 0, step[0], step[1])
    for s in range(2):
        image = cov[s] + masks[s] * signal[2 * s : 2 * s + 2]
        out[0, s] = size * direction[s]
        out[1, s] = start[s] - size * image
    finish(precv.at[pl.ds(0, NP - 1)], pss)


def shards(observed, spectra, prior_factor, noise_cov, noise_inv, sensor_block, window_len):
    any_ = pl.BlockSpec(memory_space=pl.ANY)
    dma, vmem = pltpu.SemaphoreType.DMA, pltpu.VMEM
    both = pl.pallas_call(
        kernel,
        out_shape=jax.ShapeDtypeStruct((2, 2, 2, NT), f32),
        in_specs=[any_] * 10,
        out_specs=pl.BlockSpec(memory_space=vmem),
        scratch_shapes=[
            pltpu.SMEM((2,), jnp.int32),
            pltpu.SMEM((2,), jnp.int32),
            vmem((2, 2, NT), f32),
            vmem((NS, 2, FB, 2, PD), bf16),
            vmem((NS * 16, PD), bf16),
            vmem((PD, PD), bf16),
            vmem((TP, NB, NT), bf16),
            vmem((TP, NB, NT), bf16),
            vmem((512, NT), f32),
            vmem((512, NT), f32),
            vmem((2, 512, NT), bf16),
            vmem((2, TP, NT), bf16),
            vmem((NS, 1, 128), f32),
            vmem((NS, 1, 128), f32),
            vmem((NS, 1, 128), f32),
            vmem((NS, 1, 128), f32),
            vmem((16, 128), f32),
            vmem((NP, 16, 128), f32),
            vmem((312, 512), f32),
            dma((9,)),
            dma((4,)),
        ]
        + [dma(())] * 7,
        compiler_params=pltpu.CompilerParams(
            collective_id=0, has_side_effects=True, vmem_limit_bytes=60 << 20
        ),
        cost_estimate=pl.CostEstimate(flops=10**10, bytes_accessed=10**7, transcendentals=0),
    )(
        window_len, sensor_block, observed, spectra, prior_factor,
        noise_inv.transpose(1, 0, 2), noise_cov.transpose(1, 0, 2),
        *tables(),
    )
    return both[0], both[1]


def solution(mesh):
    placed = (
        P("sens", None, None),
        P(None, None, "sens", "pts"),
        P("pts", None),
        P(),
        P(),
        P("sens"),
        P("sens"),
    )
    return jax.shard_map(
        shards,
        mesh=mesh,
        in_specs=placed,
        out_specs=(P("sens", None, None), P("sens", None, None)),
        check_vma=False,
    )
```

```python
import functools
import math

import jax
import jax.numpy as jnp
import numpy as np
from jax import lax
from jax.experimental import pallas as pl
from jax.experimental.pallas import tpu as pltpu
from jax.sharding import PartitionSpec as P

MESH = pl.DeviceIdType.MESH
NT, F, PD, NB = 420, 211, 768, 4
NS, NP = 64, 16
FB = 4
NC = -(-F // FB)
TP = 432
f32, bf16 = jnp.float32, jnp.bfloat16


def chunk_of(dev):
    return (dev * NC + NS - 1) // NS


def first_bin(c):
    return jnp.minimum(FB * c, F - FB)


def is_owner(dev):
    return chunk_of(dev + 1) != chunk_of(dev)


@functools.cache
def tables():
    t = np.arange(NT)
    fwd = np.zeros((2, FB, NS, NT))
    inv = np.zeros((NS, 2, FB, NT))
    for dev in range(NS):
        c = -(-dev * NC // NS)
        if (c * NS) // NC != dev or c >= NC:
            continue
        for f in range(FB):
            bin_ = min(FB * c, F - FB) + f
            if bin_ < FB * c:
                continue
            phase = (t * bin_) % NT
            cosine = np.cos(2 * math.pi * phase / NT)
            sine = np.where(phase % (NT // 2) == 0, 0.0, np.sin(2 * math.pi * phase / NT))
            weight = (1.0 if bin_ in (0, NT // 2) else 2.0) / NT
            fwd[0, f, dev], fwd[1, f, dev] = cosine, -sine
            inv[dev, 0, f], inv[dev, 1, f] = cosine * weight, -sine * weight
    fwd = fwd.reshape(2 * FB * NS, NT)
    inv = inv.reshape(4, 16, 8, NT).transpose(0, 2, 1, 3).reshape(512, NT)
    gt = np.zeros((128, 16))
    mask = np.zeros((16, 128))
    for xk in range(2):
        for x in range(2):
            for f in range(FB):
                for s in range(2):
                    mask[xk * 8 + f * 2 + s, xk * 32 + x * 16 + f * 4 + s * 2 :][:2] = 1
                    for r in range(2):
                        m = xk * 32 + x * 16 + f * 4 + s * 2 + r
                        j = f * 4 + (x if xk == 0 else 1 - x) * 2 + r
                        gt[m, j] = 1 if xk == 0 or x == 1 else -1
    rep = np.tile(np.eye(16), (1, 32))
    pick = np.zeros((128, 512))
    for row in range(128):
        pick[row, (row // 4) * 16 : (row // 4) * 16 + 16] = 1
    fold = np.zeros((8, 128))
    for row in range(128):
        fold[row % 4, row] = 1
    small = np.zeros((440, 512))
    small[0:128] = small[128:256] = pick
    small[256:272] = rep
    small[272:288, :128] = gt.T
    small[288:304, :128] = mask
    small[304:432, :16] = gt
    small[432:436, 0:128] = small[436:440, 128:256] = fold[0:4]
    inv = np.pad(inv, ((0, 0), (0, 512 - NT)))
    return [a.astype(np.float32) for a in (fwd, inv, small)]


def parts3(x):
    a = x.astype(bf16).astype(f32)
    b = (x - a).astype(bf16).astype(f32)
    return a, b, x - a - b


def parts2(x):
    a = x.astype(bf16)
    return a, (x - a.astype(f32)).astype(bf16)


def nt_dot(a, b):
    return lax.dot_general(a, b, (((1,), (1,)), ((), ())), preferred_element_type=f32)


def kernel(
    wl_any, sb_any, obs_any, kx, prior, ninv, ncov, dft, idft, small,
    out,
    wl, sb, obs, raw, kk, prior_v, ninv_v, ncov_v, dft_v, idft_v, idft_2, tsel, hsend, hrecv, vsend, vrecv, psend, precv, small_v,
    lsem, krecv, ksend, hss, hrs, vss, vrs, pss, prs,
):
    me, mp = lax.axis_index("sens"), lax.axis_index("pts")
    mine = is_owner(me)
    my_chunk = chunk_of(me)
    at_x, in_z, in_core = (me // 2) % 8, me // 16, me % 2
    at_z = [((in_z + dz) % 4) * 16 for dz in range(4)]

    def partners(body, low=0, high=16):
        @pl.loop(low // 2, high // 2)
        def _(w):
            for half in range(2):
                u = w * 2 + half
                dc, dx = w // 4, (w % 4) * 2 + half
                base = ((at_x + dx) % 8) * 2 + (in_core + dc) % 2
                here = dc * 32 + ((8 - dx) % 8) * 4
                for dz in range(4):
                    todo = functools.partial(body, at_z[dz] + base, here + -dz % 4, u * 4 + dz, w // 2)
                    if dz == half == 0:
                        pl.when(w != 0)(todo)
                    else:
                        todo()

    def others(body):
        for k in range(1, NP):
            body((mp + k) % NP)

    barrier = pltpu.get_barrier_semaphore()
    partners(
        lambda peer, *_: pl.semaphore_signal(barrier, inc=1, device_id={"sens": peer}, device_id_type=MESH)
    )
    others(lambda peer: pl.semaphore_signal(barrier, inc=1, device_id={"pts": peer}, device_id_type=MESH))

    locals_ = [
        pltpu.make_async_copy(wl_any, wl, lsem.at[0]),
        pltpu.make_async_copy(sb_any, sb, lsem.at[1]),
        pltpu.make_async_copy(obs_any, obs, lsem.at[2]),
        pltpu.make_async_copy(ninv, ninv_v.at[pl.ds(0, NT)], lsem.at[3]),
        pltpu.make_async_copy(dft, dft_v, lsem.at[4]),
        pltpu.make_async_copy(ncov, ncov_v.at[pl.ds(0, NT)], lsem.at[5]),
        pltpu.make_async_copy(prior, prior_v, lsem.at[6]),
        pltpu.make_async_copy(small, small_v, lsem.at[7]),
        pltpu.make_async_copy(idft, idft_v, lsem.at[8]),
    ]
    for copy in locals_:
        copy.start()
    own = pltpu.make_async_copy(kx.at[:, pl.ds(first_bin(jnp.minimum(my_chunk, NC - 1)), FB)], raw.at[0], krecv.at[0])

    @pl.when(mine)
    def _():
        own.start()

    pl.semaphore_wait(barrier, NS + NP - 2)

    def remote(src, dst, send, recv, peer):
        return pltpu.make_async_remote_copy(
            src_ref=src, dst_ref=dst, send_sem=send, recv_sem=recv, device_id=peer, device_id_type=MESH
        )

    def finish(like, sem):
        pltpu.make_async_copy(like, like, sem).wait()

    def send_bins(peer, slot, there, t):
        @pl.when(is_owner(peer))
        def _():
            first = first_bin(chunk_of(peer))
            remote(kx.at[:, pl.ds(first, FB)], raw.at[there], ksend, krecv.at[t], {"sens": peer}).start()

    partners(send_bins, 0, 10)

    for copy in locals_[:4]:
        copy.wait()

    time = lax.broadcasted_iota(jnp.int32, (2, NT), 1)
    masks = [(time < wl[s]).astype(f32) for s in range(2)]
    start = [obs[s] * masks[s] for s in range(2)]

    def select(table_v):
        @pl.loop(0, TP // 16)
        def _(i):
            rows = pl.ds(pl.multiple_of(i * 16, 16), 16)
            block = table_v[rows].astype(f32)
            which = lax.broadcasted_iota(jnp.int32, block.shape, 1)
            for s in range(2):
                tsel[s, rows, :] = jnp.where(which == sb[s], block, 0.0).sum(axis=1).astype(bf16)

    def apply_selected(x):
        out = []
        for s in range(2):
            a, b, c = parts3(x[s])
            stacked = jnp.concatenate([a, b, c, jnp.zeros_like(a)], axis=0).astype(bf16)
            y = nt_dot(stacked, tsel[s])[:, :NT]
            out.append(masks[s] * (y[0:2] + y[2:4] + y[4:6]))
        return out

    select(ninv_v)
    direction = apply_selected(start)

    locals_[4].wait()
    d4 = jnp.concatenate(direction, axis=0)
    da, db, dc = parts3(d4)
    d128 = jnp.concatenate([da] * 8 + [db] * 8 + [dc] * 8 + [jnp.zeros_like(da)] * 8, axis=0).astype(bf16)
    lane = lax.broadcasted_iota(jnp.int32, (NS, 128), 1)
    hat = jnp.zeros((NS, 128), f32)
    for part, table in enumerate(parts2(dft_v[...])):
        full = nt_dot(table, d128)
        picked = jnp.zeros((NS, 128), f32)
        for xf in range(8):
            picked += jnp.where((lane % 32) // 4 == xf, full[xf * NS : (xf + 1) * NS], 0.0)
        hat += picked + pltpu.roll(picked, 96, 1)
        if part == 0:
            hat += pltpu.roll(picked, 64, 1)
    hat = jnp.where(lane < 32, hat, 0.0)
    hsend[...] = hat.reshape(NS, 1, 128)

    def send_hat(peer, slot, there, t):
        @pl.when(is_owner(peer))
        def _():
            remote(hsend.at[peer], hrecv.at[there], hss, hrs, {"sens": peer}).start()

    partners(send_hat)
    partners(send_bins, 10, 16)
    hrecv[0] = hsend[me]

    locals_[5].wait()
    select(ncov_v)
    cov = apply_selected(direction)
    inner = sum(jnp.sum(start[s] * direction[s], axis=1, keepdims=True) for s in range(2))
    curve = sum(jnp.sum(cov[s] * direction[s], axis=1, keepdims=True) for s in range(2))
    for copy in locals_[6:]:
        copy.wait()
    idft_2[:, 0:512], idft_2[:, 512:1024] = parts2(idft_v[...])
    rep_2 = small_v[256:272].astype(bf16)
    fold_2 = small_v[432:440, 0:256].astype(bf16)

    lane1 = lax.broadcasted_iota(jnp.int32, (1, 128), 1)
    known = jnp.zeros((1, 128), f32)
    for at, value in ((34, inner[0:1]), (35, inner[1:2]), (36, curve[0:1]), (37, curve[1:2])):
        known += jnp.where(lane1 == at, value, 0.0)
    mask16 = small_v[288:304, 0:128]

    @pl.when(mine)
    def _():
        finish(hrecv.at[pl.ds(0, NS - 1)], hrs)
        rows = hrecv[...]
        twice = rows + pltpu.roll(rows.reshape(NS, 128), 32, 1).reshape(NS, 1, 128)
        z = (jnp.broadcast_to(twice, (NS, 16, 128)) * mask16[None]).reshape(NS * 16, 128).astype(bf16)
        h = nt_dot(small_v[272:288, 0:128].astype(bf16), z).astype(bf16)

        adjoint = jnp.zeros((16, PD), f32)
        for t in range(4):
            finish(raw.at[pl.ds(t * 16, 16)], krecv.at[t])

            @pl.loop(0, 16, unroll=4)
            def _(i):
                slot = t * 16 + i
                kk[pl.ds(pl.multiple_of(slot * 16, 16), 16), :] = raw[slot].reshape(16, PD)

            rows_t = slice(t * 256, t * 256 + 256)
            adjoint += jnp.dot(h[:, rows_t], kk[rows_t, :], preferred_element_type=f32)
        adjoint = adjoint.astype(bf16)
        weighted = jnp.dot(adjoint, prior_v[...], preferred_element_type=f32).astype(bf16)
        spread = nt_dot(weighted, prior_v[...]).astype(bf16)
        spread = jnp.dot(small_v[304:432, 0:16].astype(bf16), spread, preferred_element_type=f32).astype(bf16)
        cross = nt_dot(kk[...], spread)
        folded = (cross.reshape(NS, 16, 128) * mask16[None]).sum(axis=1)
        folded = folded + pltpu.roll(folded, 96, 1)
        folded = jnp.where(lane < 32, folded, 0.0)
        bins = first_bin(my_chunk) + (lane % 16) // 4
        weight = jnp.where((bins == 0) | (bins == NT // 2), 1.0, 2.0) / NT
        terms = folded * rows.reshape(NS, 128) * weight
        for r in range(2):
            value = jnp.sum(jnp.where(lane % 2 == r, terms, 0.0), keepdims=True)
            folded = folded + jnp.where(lane == 32 + r, value, 0.0)
        vsend[...] = (folded + known).reshape(NS, 1, 128)

    @pl.when(jnp.logical_not(mine))
    def _():
        vsend[...] = jnp.broadcast_to(known[None], (NS, 1, 128))

    partners(lambda peer, slot, there, t: remote(vsend.at[slot], vrecv.at[me], vss, vrs, {"sens": peer}).start())
    vrecv[me] = vsend[0]

    for is_mine, count in ((mine, NC - 1), (jnp.logical_not(mine), NC)):

        @pl.when(is_mine)
        def _():
            finish(raw.at[pl.ds(0, count)], ksend)
            finish(hsend.at[pl.ds(0, count)], hss)

    finish(vrecv.at[pl.ds(0, NS - 1)], vrs)

    got = vrecv[...].reshape(NS, 128)
    total = jnp.sum(got, axis=0, keepdims=True)
    got = jnp.where(lane < 32, got, 0.0)
    packed = got[0:16]
    for q in range(1, 4):
        packed += pltpu.roll(got[16 * q : 16 * q + 16], 32 * q, 1)
    row16 = lax.broadcasted_iota(jnp.int32, (16, 128), 0)
    lane16 = lax.broadcasted_iota(jnp.int32, (16, 128), 1)
    spare = jnp.broadcast_to(pltpu.roll(jnp.where((lane1 == 32) | (lane1 == 33), total, 0.0), 64, 1), (16, 128))
    packed = jnp.where((row16 == 15) & (lane16 >= 96), spare, packed)
    psend[...] = packed
    others(lambda peer: remote(psend, precv.at[mp], pss, prs, {"pts": peer}).start())
    precv[mp] = packed
    finish(vsend.at[pl.ds(0, NS - 1)], vss)
    finish(precv.at[pl.ds(0, NP - 1)], prs)
    forward = jnp.sum(precv[...], axis=0)

    def at_lane(x, n):
        return jnp.sum(jnp.where(lax.broadcasted_iota(jnp.int32, x.shape, 1) == n, x, 0.0), axis=1, keepdims=True)

    last = forward[15:16]
    step = [at_lane(total, 34 + r) / (at_lane(last, 96 + r) + at_lane(total, 36 + r)) for r in range(2)]
    fine = jnp.concatenate(parts2(forward), axis=1)
    tiled = lax.dot_general(fine, rep_2, (((0,), (0,)), ((), ())), preferred_element_type=f32)
    tiled = (tiled * small_v[0:256]).astype(bf16)
    both = jnp.dot(fold_2, tiled, preferred_element_type=f32).astype(bf16)
    full = jnp.dot(both, idft_2[...], preferred_element_type=f32)
    signal = full[0:4, 0:NT] + full[4:8, 0:NT] + full[0:4, 512 : 512 + NT]
    row2 = lax.broadcasted_iota(jnp.int32, (2, NT), 0)
    size = jnp.where(row2 == 0, step[0], step[1])
    for s in range(2):
        image = cov[s] + masks[s] * signal[2 * s : 2 * s + 2]
        out[0, s] = size * direction[s]
        out[1, s] = start[s] - size * image
    finish(precv.at[pl.ds(0, NP - 1)], pss)


def shards(observed, spectra, prior_factor, noise_cov, noise_inv, sensor_block, window_len):
    hbm = pl.BlockSpec(memory_space=pltpu.HBM)
    dma, vmem = pltpu.SemaphoreType.DMA, pltpu.VMEM
    both = pl.pallas_call(
        kernel,
        out_shape=jax.ShapeDtypeStruct((2, 2, 2, NT), f32),
        in_specs=[hbm] * 10,
        out_specs=pl.BlockSpec(memory_space=vmem),
        scratch_shapes=[
            pltpu.SMEM((2,), jnp.int32),
            pltpu.SMEM((2,), jnp.int32),
            vmem((2, 2, NT), f32),
            vmem((NS, 2, FB, 2, PD), bf16),
            vmem((NS * 16, PD), bf16),
            vmem((PD, PD), bf16),
            vmem((TP, NB, NT), bf16),
            vmem((TP, NB, NT), bf16),
            vmem((512, NT), f32),
            vmem((512, 512), f32),
            vmem((512, 1024), bf16),
            vmem((2, TP, NT), bf16),
            vmem((NS, 1, 128), f32),
            vmem((NS, 1, 128), f32),
            vmem((NS, 1, 128), f32),
            vmem((NS, 1, 128), f32),
            vmem((16, 128), f32),
            vmem((NP, 16, 128), f32),
            vmem((440, 512), f32),
            dma((9,)),
            dma((4,)),
        ]
        + [dma(())] * 7,
        compiler_params=pltpu.CompilerParams(
            collective_id=0, has_side_effects=True, vmem_limit_bytes=60 << 20
        ),
        cost_estimate=pl.CostEstimate(flops=10**10, bytes_accessed=10**7, transcendentals=0),
    )(
        window_len, sensor_block, observed, spectra, prior_factor,
        noise_inv.transpose(1, 0, 2), noise_cov.transpose(1, 0, 2),
        *tables(),
    )
    return both[0], both[1]


def solution(mesh):
    placed = (
        P("sens", None, None),
        P(None, None, "sens", "pts"),
        P("pts", None),
        P(),
        P(),
        P("sens"),
        P("sens"),
    )
    return jax.shard_map(
        shards,
        mesh=mesh,
        in_specs=placed,
        out_specs=(P("sens", None, None), P("sens", None, None)),
        check_vma=False,
    )
```
